32 devices in a mesh: rep: 2 (over x), node: 4 (over y, core), tp: 4 (over z).
Axes of the slice: x: 2, y: 2, z: 4, core: 2. Of those that a mesh axis runs over, the one named last changes fastest.
Arguments:
- queries: bfloat16 [256, 6144], P(('rep', 'node'), 'tp'), parts along dimension 0, may hold values from -130 to 130
- cache_keys: bfloat16 [256, 8, 384, 128], P(('rep', 'node'), 'tp'), parts along dimension 0, may hold values from -6 to 6
- cache_values: bfloat16 [256, 8, 384, 128], P(('rep', 'node'), 'tp'), parts along dimension 0, may hold values from -6 to 6
- new_keys: bfloat16 [256, 1024], P(('rep', 'node'), 'tp'), parts along dimension 0, may hold values from -6 to 6
- new_values: bfloat16 [256, 1024], P(('rep', 'node'), 'tp'), parts along dimension 0, may hold values from -6 to 6
- lengths: int32 [256], P(('rep', 'node')), parts along dimension 0, may hold values from 2 to 384, as said below
- resid: bfloat16 [256, 6144], P(('rep', 'tp'), 'node'), parts along dimension 0, may hold values from -80 to 80
- wo: bfloat16 [6144, 6144], P('tp', 'node'), may hold values from -0.078125 to 0.078125
- norm_gain: float32 [6144], P('node'), may hold values from 0.1 to 1.9
- routes: int32 [256, 2], P('rep'), parts along dimension 0, may hold values from 0 to 3, all different within a row; in each aligned block of 128 rows (0 to 127, 128 to 255, ...) at most 80 rows name the same one
- route_weights: float32 [256, 2], P('rep'), parts along dimension 0, may hold values from 0.2 to 1
- w_gate: bfloat16 [6144, 32768], P(None, ('node', 'tp')), may hold values from -0.078125 to 0.078125
- w_up: bfloat16 [6144, 32768], P(None, ('node', 'tp')), may hold values from -0.078125 to 0.078125
- w_down: bfloat16 [32768, 6144], P(('node', 'tp')), may hold values from -0.09375 to 0.09375
Outputs:
- mixed: bfloat16 [256, 6144], P(('rep', 'tp'), 'node'), parts along dimension 0
The draws below stay inside these ranges and needn't reach their ends.
There are 2 independent parts, one for each index of `rep`. The reference program is written for one: setup_inputs(seed, part) draws one part's arguments, and reference() takes and returns one part's arrays. A program takes and returns all parts, laid end to end along the dimension named above; an argument that names none is the same for every part. Nothing has to cross between parts.
Inputs may be any that keep to these rules, and one draw needn't show every extreme that they name: `routes`: each row names two different experts; over all 128 rows no expert is named by more than 80 rows, a bound that some block reaches. `lengths`: row 0 has exactly 384.
All inputs are finite; a program needn't handle non-finite values.
Results may differ from the reference program's by a relative error of at most 0.005.
Values may be sent and summed in bfloat16 or wider, within the bound.
A program may use at most 192 MiB of HBM per device.

```python
import math
import jax
import jax.numpy as jnp
import numpy as np
from jax import lax

D = 6144
HQ = 48
KVH = 8
HD = 128
EXPERTS = 4
FF = 8192
CTX = 384
TOKENS = 128
CAPT = 80


def shared_keys(key):
    return jnp.clip(jax.random.normal(key, (TOKENS, KVH, CTX, HD), jnp.float32), -6.0, 6.0)


def draw_cache_keys(key, part):
    base = shared_keys(key)
    return base.astype(jnp.bfloat16)


def draw_queries(key, part):
    key = jax.random.fold_in(key, 22)
    first = jax.random.fold_in(key, 0)
    base = jnp.clip(jax.random.normal(first, (TOKENS, HQ, HD), jnp.float32), -6.0, 6.0)
    return base.reshape(TOKENS, HQ * HD).astype(jnp.bfloat16)


def draw_lengths(key, part):
    key = jax.random.fold_in(key, 23)
    drawn = jax.random.randint(key, (TOKENS,), 2, CTX + 1, dtype=jnp.int32)
    return drawn.at[0].set(CTX)


def draw_resid(key, part):
    key = jax.random.fold_in(key, 24)
    first = jax.random.fold_in(key, 0)
    base = jnp.clip(jax.random.normal(first, (TOKENS, D), jnp.float32), -6.0, 6.0)
    columns = 1.0 + 2.0 * jnp.arange(D, dtype=jnp.float32) / D
    base = base * columns[None, :]
    return base.astype(jnp.bfloat16)


def strengthened(values, stream_key, source, target, blocks, factor):
    owner, partner = [(jnp.arange(values.shape[axis_at]) // (values.shape[axis_at] // blocks)).reshape([-1 if axis == axis_at else 1 for axis in range(values.ndim)]) for axis_at in (source, target)]
    chosen = jax.random.permutation(stream_key, blocks)[partner]
    strong = (owner == chosen) | (owner == (partner + blocks // 2) % blocks)
    return jnp.where(strong, factor * values, values)


def steps_of(stream_key, dims, shards, smallest, top_value):
    factor_of = 1.0
    for axis_at, blocks in shards:
        heights = jax.random.uniform(jax.random.fold_in(jax.random.fold_in(stream_key, 6), axis_at), (blocks,), jnp.float32, smallest / len(shards), top_value / len(shards))
        factor_of = factor_of * jnp.repeat(jnp.exp(heights), dims[axis_at] // blocks).reshape((-1,) + (1,) * (len(dims) - 1 - axis_at))
    return factor_of


def routed_block(key, own, number, rows, amount, top, limit, slope):
    sequence = jax.random.permutation(key, amount)
    packed, ordinary = load_shares(amount, rows * top, limit, slope, True), load_shares(amount, rows * top, limit, slope, False)
    places = jnp.arange(amount)

    def named(sizes, turn):
        used = int((sizes > 0).sum())
        fixed = max(1, used // 4)
        shifted = fixed + (places - fixed + turn * (used - fixed)) % max(1, amount - fixed)
        return jnp.zeros((amount,), jnp.int32).at[sequence[jnp.where(places < fixed, places, shifted)]].set(jnp.asarray(sizes, jnp.int32))

    sizes = jnp.where(number % 4 == 0, named(packed, number // 4), named(ordinary, number - number // 4 - 1))
    mixed = jax.random.permutation(jax.random.fold_in(own, 3), amount)
    source_of, taker = mixed[0:amount // 2 * 2:2], mixed[1:amount // 2 * 2:2]
    slack = jnp.minimum(sizes[source_of] - 1, limit - sizes[taker]) // 2
    slack = jnp.where((source_of == sequence[0]) | (taker == sequence[0]) | (sizes[taker] == 0), 0, jnp.maximum(slack, 0))
    shifted = jax.random.randint(jax.random.fold_in(own, 4), (amount // 2,), 0, 1 << 20) % (slack + 1)
    sizes = sizes.at[source_of].add(-shifted).at[taker].add(shifted)
    members = jnp.searchsorted(jnp.cumsum(sizes), jnp.arange(rows * top), side="right").astype(jnp.int32)
    listing = members.reshape(top, rows).T
    listing = listing[jax.random.permutation(jax.random.fold_in(own, 1), rows)]
    turn = jax.random.randint(jax.random.fold_in(own, 2), (rows, 1), 0, top)
    return jnp.take_along_axis(listing, (jnp.arange(top)[None, :] + turn) % top, axis=1)


def load_shares(amount, total, reach, slope, full):
    loads = [(1 << 20) // math.isqrt(standing ** slope) + 1 for standing in range(1, amount + 1)]
    largest = reach if full else min(reach, max(-(-total // amount), total * loads[0] // sum(loads)))
    least = 1 if total - largest >= amount - 1 else 0
    counts, surplus = [largest] + [least] * (amount - 1), total - largest - least * (amount - 1)
    while surplus > 0:
        candidates = [i for i in range(1, amount) if counts[i] < largest] or [i for i in range(1, amount) if counts[i] < reach]
        whole, remaining = sum([loads[i] for i in candidates]), surplus
        for i in candidates:
            more = min(reach - counts[i], max(1, remaining * loads[i] // whole), surplus)
            counts[i] = counts[i] + more
            surplus = surplus - more
    return np.array(counts)


def centred(own_key, dims, width, most, pieces=(), kind=jnp.bfloat16):
    entries = width * jax.random.normal(own_key, dims, jnp.float32)
    if pieces:
        entries = entries * steps_of(own_key, dims, pieces, -0.22, 0.18)
    return jnp.clip(entries, -most, most).astype(kind)


def bell_draw_with(rng, extent, width, limit, pieces, heavy, kind=jnp.bfloat16):
    array = width * jax.random.normal(rng, extent, jnp.float32)
    if pieces:
        array = array * steps_of(rng, extent, pieces, -0.22, 0.18)
    return jnp.clip(strengthened(array, jax.random.fold_in(rng, 3), *heavy), -limit, limit).astype(kind)


def setup_inputs(seed: int = 0, part: int = 0) -> dict:
    key_list = jax.random.split(jax.random.key(seed), 15)
    part_keys = jax.random.split(jax.random.fold_in(key_list[14], part), 15)
    queries = draw_queries(jax.random.fold_in(jax.random.fold_in(key_list[14], part), 71), part)
    cache_keys = draw_cache_keys(jax.random.fold_in(jax.random.fold_in(key_list[14], part), 71), part)
    cache_values = centred(part_keys[2], (TOKENS, KVH, CTX, HD), 1.0, 6.0, ((0, 4), (1, 4)))
    new_keys = centred(part_keys[3], (TOKENS, KVH * HD), 1.0, 6.0, ((0, 4), (1, 4)))
    new_values = centred(part_keys[4], (TOKENS, KVH * HD), 1.0, 6.0, ((0, 4), (1, 4)))
    lengths = draw_lengths(jax.random.fold_in(jax.random.fold_in(key_list[14], part), 71), part)
    resid = draw_resid(jax.random.fold_in(jax.random.fold_in(key_list[14], part), 71), part)
    wo = centred(key_list[7], (HQ * HD, D), (HQ * HD) ** -0.5, 0.078125, ((0, 4), (1, 4)))
    norm_gain = jnp.clip(1.0 + 0.18 * jax.random.normal(key_list[8], (D,), jnp.float32), 0.1, 1.9)
    routes_keys = jax.random.split(jax.random.fold_in(part_keys[9], 1), TOKENS // TOKENS)
    routes_turns = jax.random.permutation(jax.random.fold_in(part_keys[9], 3), TOKENS // TOKENS)
    routes = jax.vmap(lambda own, number: routed_block(jax.random.fold_in(part_keys[9], 2), own, number, TOKENS, EXPERTS, 2, CAPT, 1))(routes_keys, routes_turns).reshape((TOKENS, 2))
    route_weights = jnp.clip(jax.random.uniform(part_keys[10], (TOKENS, 2), jnp.float32, 0.2, 1.0), 0.2, 1.0)
    w_gate = centred(key_list[11], (D, EXPERTS * FF), D ** -0.5, 0.078125, ((1, 16),))
    w_up = centred(key_list[12], (D, EXPERTS * FF), D ** -0.5, 0.078125, ((1, 16),))
    w_down = bell_draw_with(key_list[13], (EXPERTS * FF, D), FF ** -0.5, 0.09375, ((0, 16),), (0, 1, 16, 2.0))
    return dict(queries=queries, cache_keys=cache_keys, cache_values=cache_values, new_keys=new_keys, new_values=new_values, lengths=lengths, resid=resid, wo=wo, norm_gain=norm_gain, routes=routes, route_weights=route_weights, w_gate=w_gate, w_up=w_up, w_down=w_down)


EPSILON = 1e-05

def attend_row(items):
    query_row, keys_row, values_row, key_new, value_new, length = items
    groups = HQ // KVH
    factor = HD ** (-0.5)
    query_heads = query_row.astype(jnp.float32).reshape(KVH, groups, HD)
    scores = jnp.einsum('kgd,kpd->kgp', query_heads, keys_row.astype(jnp.float32)) * factor
    valid = jnp.arange(CTX, dtype=jnp.int32) < length
    scores = jnp.where(valid[None, None, :], scores, -jnp.inf)
    score_new = jnp.einsum('kgd,kd->kg', query_heads, key_new.reshape(KVH, HD).astype(jnp.float32)) * factor
    highest = jnp.maximum(lax.optimization_barrier(jnp.max(scores, axis=-1)), score_new)
    exp_cache = jnp.exp(scores - highest[..., None])
    exp_new = jnp.exp(score_new - highest)
    totals = lax.optimization_barrier(jnp.sum(exp_cache, axis=-1)) + exp_new
    probs_cache = lax.optimization_barrier((exp_cache / totals[..., None]).astype(jnp.bfloat16))
    probs_new = lax.optimization_barrier((exp_new / totals).astype(jnp.bfloat16))
    attended = jnp.einsum('kgp,kpd->kgd', probs_cache.astype(jnp.float32), values_row.astype(jnp.float32))
    attended = attended + probs_new.astype(jnp.float32)[..., None] * value_new.reshape(KVH, 1, HD).astype(jnp.float32)
    return attended.reshape(HQ * HD).astype(jnp.bfloat16)

def reference(queries, cache_keys, cache_values, new_keys, new_values, lengths, resid, wo, norm_gain, routes, route_weights, w_gate, w_up, w_down):
    attended = lax.map(attend_row, (queries, cache_keys, cache_values, new_keys, new_values, lengths))
    projected = jnp.dot(attended, wo, preferred_element_type=jnp.float32)
    hidden = resid.astype(jnp.float32) + projected
    mean_square = lax.optimization_barrier(jnp.mean(hidden * hidden, axis=1, keepdims=True))
    normed = (hidden * lax.rsqrt(mean_square + EPSILON) * norm_gain[None, :]).astype(jnp.bfloat16)
    moe_sum = jnp.zeros(hidden.shape, jnp.float32)
    for expert in range(EXPERTS):
        weight_e = lax.optimization_barrier(jnp.sum(jnp.where(routes == expert, route_weights, 0.0), axis=1))
        gate = jnp.dot(normed, w_gate[:, expert * FF:(expert + 1) * FF], preferred_element_type=jnp.float32)
        upward = jnp.dot(normed, w_up[:, expert * FF:(expert + 1) * FF], preferred_element_type=jnp.float32)
        activ = (jax.nn.silu(gate) * upward).astype(jnp.bfloat16)
        output_e = jnp.dot(activ, w_down[expert * FF:(expert + 1) * FF, :], preferred_element_type=jnp.float32)
        moe_sum = moe_sum + weight_e[:, None] * output_e
    return (hidden + moe_sum).astype(jnp.bfloat16)
```

```python
import functools

import jax
import jax.numpy as jnp
from jax import lax
from jax.experimental import pallas as pl
from jax.experimental.pallas import tpu as pltpu
from jax.sharding import PartitionSpec as P

D = 6144
HQ = 48
KVH = 8
HD = 128
FF = 8192
CTX = 384


EPSILON = 1e-05


def attend_block(queries, cache_keys, cache_values, new_keys, new_values, lengths):
    rows, kv_local = (cache_keys.shape[0], cache_keys.shape[1])
    groups = HQ // KVH
    factor = HD ** (-0.5)
    query_heads = queries.reshape(rows, kv_local, groups, HD)
    scores = (
        jnp.einsum("rkgd,rkpd->rkgp", query_heads, cache_keys, preferred_element_type=jnp.float32)
        * factor
    )
    valid = jnp.arange(CTX, dtype=jnp.int32)[None, :] < lengths[:, None]
    scores = jnp.where(valid[:, None, None, :], scores, -jnp.inf)
    key_heads = new_keys.reshape(rows, kv_local, HD)
    score_new = (
        jnp.einsum("rkgd,rkd->rkg", query_heads, key_heads, preferred_element_type=jnp.float32)
        * factor
    )
    highest = jnp.maximum(jnp.max(scores, axis=-1), score_new)
    exp_cache = jnp.exp(scores - highest[..., None])
    exp_new = jnp.exp(score_new - highest)
    totals = jnp.sum(exp_cache, axis=-1) + exp_new
    probs_cache = (exp_cache / totals[..., None]).astype(jnp.bfloat16)
    probs_new = (exp_new / totals).astype(jnp.bfloat16)
    attended = jnp.einsum(
        "rkgp,rkpd->rkgd", probs_cache, cache_values, preferred_element_type=jnp.float32
    )
    attended = attended + probs_new.astype(jnp.float32)[..., None] * new_values.reshape(
        rows, kv_local, 1, HD
    ).astype(jnp.float32)
    return attended.reshape(rows, kv_local * groups * HD).astype(jnp.bfloat16)


DEPTH = 2048
CHUNK = 512
MESH = pl.DeviceIdType.MESH


def layer_kernel(
    T,
    att_ref,
    resid_ref,
    gain_ref,
    routes_ref,
    rw_ref,
    wo_hbm,
    wg_hbm,
    wu_hbm,
    wd_hbm,
    out_ref,
    w_buf,
    att_all,
    full,
    hidden,
    act,
    acc,
    proj_send,
    proj_recv,
    sq_node,
    sq_all,
    sib_send,
    sib_recv,
    y_send,
    y_recv,
    z_recv,
    w_sem,
    att_s,
    att_r,
    pr_s,
    pr_r,
    sqn_s,
    sqn_r,
    sqt_s,
    sqt_r,
    ag_z_s,
    ag_y_s,
    ag_c_s,
    ag_r,
    sib_s,
    sib_r,
    y_s,
    y_r,
    z_s,
    z_r,
):
    N = 4
    R, F = resid_ref.shape
    r = lax.axis_index("rep")
    n = lax.axis_index("node")
    t = lax.axis_index("tp")
    y = n // 2
    core = n % 2
    ny = (n + 2) % N
    ns = y * 2 + (core + 1) % 2
    nd = (ns + 2) % N
    SLOTS = w_buf.shape[0]
    KB = D // DEPTH
    per_c = 2 * KB
    chunks = wg_hbm.shape[1] // CHUNK
    wo_first = SLOTS - F // CHUNK

    def tpeer(d):
        return (t + d) % T

    def npeer(d):
        return (n + d) % N

    def rows(i):
        return pl.ds(pl.multiple_of(i * R, R), R)

    def feats(i):
        return pl.ds(pl.multiple_of(i * F, F), F)

    def gu_copy(slot):
        c, k = slot // per_c, slot % per_c
        hbm = wg_hbm if k < KB else wu_hbm
        return pltpu.make_async_copy(
            hbm.at[pl.ds((k % KB) * DEPTH, DEPTH), pl.ds(c * CHUNK, CHUNK)],
            w_buf.at[slot],
            w_sem.at[slot],
        )

    def dest(q):
        return ((y + 1 - q // 2) % 2) * 2 + (core + 1 - q % 2) % 2

    def down_copy(i):
        col = dest(i // (F // CHUNK)) * F + (i % (F // CHUNK)) * CHUNK
        return pltpu.make_async_copy(
            wd_hbm.at[:, pl.ds(pl.multiple_of(col, CHUNK), CHUNK)], w_buf.at[i], w_sem.at[i]
        )

    def wo_copy(j):
        return pltpu.make_async_copy(
            wo_hbm.at[:, pl.ds(j * CHUNK, CHUNK)],
            w_buf.at[wo_first + j, pl.ds(0, F)],
            w_sem.at[wo_first + j],
        )

    def remote(src, dst, ss, rs, node, tp):
        return pltpu.make_async_remote_copy(
            src_ref=src,
            dst_ref=dst,
            send_sem=ss,
            recv_sem=rs,
            device_id=(r, node, tp),
            device_id_type=MESH,
        )

    for j in range(F // CHUNK):
        wo_copy(j).start()
    for slot in range(wo_first):
        gu_copy(slot).start()

    barrier = pltpu.get_barrier_semaphore()
    for d in range(1, N):
        pl.semaphore_signal(barrier, inc=1, device_id=(r, npeer(d), t), device_id_type=MESH)
    for d in range(1, T):
        pl.semaphore_signal(barrier, inc=1, device_id=(r, n, tpeer(d)), device_id_type=MESH)
    pl.semaphore_wait(barrier, N + T - 2)

    sends = []

    def send(*args):
        copy = remote(*args)
        copy.start()
        sends.append(copy)

    for d in (2, 1, 3):
        send(att_ref, att_all.at[rows(n)], att_s.at[d], att_r.at[n], npeer(d), t)
    att_all[rows(n), :] = att_ref[...]
    for d in range(1, N):
        p = npeer(d)
        remote(att_ref, att_all.at[rows(p)], att_s.at[d], att_r.at[p], p, t).wait_recv()

    for j in range(F // CHUNK):
        wo_copy(j).wait()
        part = jnp.dot(
            att_all[...], w_buf[wo_first + j, :F, :], preferred_element_type=jnp.float32
        )
        acc[:, j * CHUNK : (j + 1) * CHUNK] = part
        proj_send[:, j * CHUNK : (j + 1) * CHUNK] = part.astype(jnp.bfloat16)
    for d in (2, 1, 3):
        p = tpeer(d)
        send(proj_send.at[rows(p)], proj_recv.at[t], pr_s.at[d], pr_r.at[t], n, p)
    for slot in range(wo_first, SLOTS):
        gu_copy(slot).start()
    total = resid_ref[...].astype(jnp.float32) + acc[rows(t), :]
    for d in range(1, T):
        p = tpeer(d)
        remote(
            proj_send.at[rows(p)], proj_recv.at[p], pr_s.at[d], pr_r.at[p], n, p
        ).wait_recv()
        total = total + proj_recv[p].astype(jnp.float32)
    hidden[...] = total

    full[rows(t), feats(n)] = (total * gain_ref[...]).astype(jnp.bfloat16)
    sq_node[n] = jnp.broadcast_to(jnp.sum(total * total, axis=1, keepdims=True), (R, 128))
    for d in range(1, N):
        send(sq_node.at[n], sq_node.at[n], sqn_s.at[d], sqn_r.at[n], npeer(d), t)

    def block(nn, tt):
        return full.at[rows(tt), feats(nn)]

    own = block(n, t)
    send(own, own, ag_y_s.at[0], ag_r.at[n, t], ny, t)
    for d in (2, 1, 3):
        send(own, own, ag_z_s.at[d], ag_r.at[n, t], n, tpeer(d))
    send(own, own, ag_c_s.at[0, 0], ag_r.at[n, t], ns, t)

    for d in range(1, N):
        p = npeer(d)
        remote(sq_node.at[n], sq_node.at[p], sqn_s.at[d], sqn_r.at[p], p, t).wait_recv()
    sq_all[rows(t), :] = sq_node[0] + sq_node[1] + sq_node[2] + sq_node[3]
    for d in range(1, T):
        sq = sq_all.at[rows(t)]
        send(sq, sq, sqt_s.at[d], sqt_r.at[t], n, tpeer(d))

    def arrived(nn, tt):
        remote(own, block(nn, tt), ag_y_s.at[0], ag_r.at[nn, tt], ny, t).wait_recv()

    for d in (1, 3, 2):
        p = tpeer(d)
        b = block(n, p)
        arrived(n, p)
        send(b, b, ag_y_s.at[d], ag_r.at[n, p], ny, t)
        send(b, b, ag_c_s.at[0, d], ag_r.at[n, p], ns, t)
    for d in (0, 1, 3, 2):
        p = tpeer(d)
        b = block(ny, p)
        arrived(ny, p)
        send(b, b, ag_c_s.at[1, d], ag_r.at[ny, p], ns, t)
    for d in range(T):
        arrived(ns, tpeer(d))
        arrived(nd, tpeer(d))
    for d in range(1, T):
        p = tpeer(d)
        sq = sq_all.at[rows(p)]
        remote(sq, sq, sqt_s.at[d], sqt_r.at[p], n, p).wait_recv()
    inv = lax.rsqrt(sq_all[:, 0:1] / D + EPSILON)

    def slot_wait(slot):
        pltpu.make_async_copy(
            wd_hbm.at[:, pl.ds(0, CHUNK)], w_buf.at[slot], w_sem.at[slot]
        ).wait()

    downs = D // CHUNK

    def gate_up(c, carry):
        base = c * per_c
        both = []
        for m in range(2):
            s = None
            for k in range(KB):
                slot = base + m * KB + k
                slot_wait(slot)
                part = jnp.dot(
                    full[:, k * DEPTH : (k + 1) * DEPTH],
                    w_buf[slot],
                    preferred_element_type=jnp.float32,
                )
                s = part if s is None else s + part
            both.append(s * inv)
        gate, up = both
        act[:, pl.ds(pl.multiple_of(c * CHUNK, CHUNK), CHUNK)] = (
            gate / (1.0 + jnp.exp(-gate)) * up
        ).astype(jnp.bfloat16)

        @pl.when(c < downs // per_c)
        def _():
            for k in range(per_c):
                down_copy(base + k).start()

        return carry

    lax.fori_loop(0, chunks, gate_up, 0)

    expert = (n * T + t) * wg_hbm.shape[1] // FF
    weight = jnp.sum(jnp.where(routes_ref[...] == expert, rw_ref[...], 0.0), axis=1, keepdims=True)

    def down(q, store):
        def step(k, carry):
            slot = q * (F // CHUNK) + k
            slot_wait(slot)
            part = jnp.dot(act[...], w_buf[slot], preferred_element_type=jnp.float32)
            store(pl.ds(pl.multiple_of(k * CHUNK, CHUNK), CHUNK), part * weight)
            return carry

        lax.fori_loop(0, F // CHUNK, step, 0)

    def to_sibling(h):
        def store(cols, v):
            sib_send[h, :, cols] = v.astype(jnp.bfloat16)

        return store

    def to_acc(cols, v):
        acc[:, cols] = v

    def sib_wait(h):
        remote(
            sib_send.at[h], sib_recv.at[h], sib_s.at[h], sib_r.at[h], ns, t
        ).wait_recv()

    down(0, to_sibling(0))
    send(sib_send.at[0], sib_recv.at[0], sib_s.at[0], sib_r.at[0], ns, t)
    down(1, to_acc)
    sib_wait(0)
    for d in (2, 1, 3, 0):
        p = tpeer(d)
        y_send[p] = (acc[rows(p), :] + sib_recv[0, rows(p), :].astype(jnp.float32)).astype(
            jnp.bfloat16
        )
        send(y_send.at[p], y_recv.at[p], y_s.at[d], y_r.at[p], ny, t)
    down(2, to_sibling(1))
    send(sib_send.at[1], sib_recv.at[1], sib_s.at[1], sib_r.at[1], ns, t)
    down(3, to_acc)
    sib_wait(1)
    mine = None
    for d in (2, 1, 3, 0):
        p = tpeer(d)
        remote(y_send.at[p], y_recv.at[p], y_s.at[d], y_r.at[p], ny, t).wait_recv()
        s = (
            acc[rows(p), :]
            + sib_recv[1, rows(p), :].astype(jnp.float32)
            + y_recv[p].astype(jnp.float32)
        )
        if d == 0:
            mine = s + hidden[...]
        else:
            y_recv[p] = s.astype(jnp.bfloat16)
            send(y_recv.at[p], z_recv.at[t], z_s.at[d], z_r.at[t], n, p)
    for d in (1, 3, 2):
        p = tpeer(d)
        remote(y_recv.at[p], z_recv.at[p], z_s.at[d], z_r.at[p], n, p).wait_recv()
        mine = mine + z_recv[p].astype(jnp.float32)
    out_ref[...] = mine.astype(jnp.bfloat16)
    for copy in sends:
        copy.wait_send()


def fused_layer(
    attended, resid, wo, norm_gain, routes, route_weights, w_gate, w_up, w_down, tp
):
    R, F = resid.shape
    rows = routes.shape[0]
    bf, f32 = jnp.bfloat16, jnp.float32
    vm = pl.BlockSpec(memory_space=pltpu.VMEM)
    hbm = pl.BlockSpec(memory_space=pl.ANY)
    slots = 2 * (D // DEPTH) * (w_gate.shape[1] // CHUNK)
    dma = pltpu.SemaphoreType.DMA
    return pl.pallas_call(
        functools.partial(layer_kernel, tp),
        out_shape=jax.ShapeDtypeStruct((R, F), bf),
        in_specs=[vm] * 5 + [hbm] * 4,
        out_specs=vm,
        scratch_shapes=[
            pltpu.VMEM((slots, DEPTH, CHUNK), bf),
            pltpu.VMEM((rows, F), bf),
            pltpu.VMEM((rows, D), bf),
            pltpu.VMEM((R, F), f32),
            pltpu.VMEM((rows, w_gate.shape[1]), bf),
            pltpu.VMEM((rows, F), f32),
            pltpu.VMEM((rows, F), bf),
            pltpu.VMEM((tp, R, F), bf),
            pltpu.VMEM((4, R, 128), f32),
            pltpu.VMEM((rows, 128), f32),
            pltpu.VMEM((2, rows, F), bf),
            pltpu.VMEM((2, rows, F), bf),
            pltpu.VMEM((tp, R, F), bf),
            pltpu.VMEM((tp, R, F), bf),
            pltpu.VMEM((tp, R, F), bf),
            dma((slots,)),
            dma((4,)),
            dma((4,)),
            dma((tp,)),
            dma((tp,)),
            dma((4,)),
            dma((4,)),
            dma((tp,)),
            dma((tp,)),
            dma((tp,)),
            dma((tp,)),
            dma((2, tp)),
            dma((4, tp)),
            dma((2,)),
            dma((2,)),
            dma((tp,)),
            dma((tp,)),
            dma((tp,)),
            dma((tp,)),
        ],
        compiler_params=pltpu.CompilerParams(
            collective_id=0, has_side_effects=True, vmem_limit_bytes=60 * 1024 * 1024
        ),
        cost_estimate=pl.CostEstimate(
            flops=2 * rows * D * w_gate.shape[1] * 3,
            bytes_accessed=3 * D * w_gate.shape[1] * 2,
            transcendentals=rows * w_gate.shape[1],
        ),
    )(
        attended,
        resid,
        norm_gain.reshape(1, F),
        routes,
        route_weights,
        wo,
        w_gate,
        w_up,
        w_down,
    )


def local(
    queries,
    cache_keys,
    cache_values,
    new_keys,
    new_values,
    lengths,
    resid,
    wo,
    norm_gain,
    routes,
    route_weights,
    w_gate,
    w_up,
    w_down,
):
    attended = attend_block(queries, cache_keys, cache_values, new_keys, new_values, lengths)
    if lax.axis_size("node") == 4 and lax.axis_size("tp") == 4:
        return fused_layer(
            attended,
            resid,
            wo,
            norm_gain,
            routes,
            route_weights,
            w_gate,
            w_up,
            w_down,
            lax.axis_size("tp"),
        )
    gathered = lax.all_gather(attended, "node", axis=0, tiled=True)
    projected = lax.psum_scatter(
        jnp.dot(gathered, wo, preferred_element_type=jnp.float32),
        "tp",
        scatter_dimension=0,
        tiled=True,
    )
    hidden = resid.astype(jnp.float32) + projected
    squares = lax.psum(jnp.sum(hidden * hidden, axis=1), "node")
    normed = (hidden * lax.rsqrt(squares / D + EPSILON)[:, None] * norm_gain[None, :]).astype(
        jnp.bfloat16
    )
    all_rows = lax.all_gather(normed, "tp", axis=0, tiled=True)
    device = lax.axis_index("node") * lax.axis_size("tp") + lax.axis_index("tp")
    hidden_local = w_gate.shape[1]
    expert = device * hidden_local // FF
    expert_weight = jnp.sum(jnp.where(routes == expert, route_weights, 0.0), axis=1)
    full_rows = lax.all_gather(all_rows, "node", axis=1, tiled=True)
    gate = jnp.dot(full_rows, w_gate, preferred_element_type=jnp.float32)
    upward = jnp.dot(full_rows, w_up, preferred_element_type=jnp.float32)
    activ = (jax.nn.silu(gate) * upward).astype(jnp.bfloat16)
    weighted = jnp.dot(activ, w_down, preferred_element_type=jnp.float32) * expert_weight[:, None]
    slices = lax.psum_scatter(
        weighted.astype(jnp.bfloat16), "node", scatter_dimension=1, tiled=True
    ).astype(jnp.float32)
    moe_part = lax.psum_scatter(slices, "tp", scatter_dimension=0, tiled=True)
    return (hidden + moe_part).astype(jnp.bfloat16)


def solution(mesh):
    return jax.shard_map(
        local,
        mesh=mesh,
        in_specs=(
            P(("rep", "node"), "tp"),
            P(("rep", "node"), "tp", None, None),
            P(("rep", "node"), "tp", None, None),
            P(("rep", "node"), "tp"),
            P(("rep", "node"), "tp"),
            P(("rep", "node")),
            P(("rep", "tp"), "node"),
            P("tp", "node"),
            P("node"),
            P("rep", None),
            P("rep", None),
            P(None, ("node", "tp")),
            P(None, ("node", "tp")),
            P(("node", "tp"), None),
        ),
        out_specs=P(("rep", "tp"), "node"),
        check_vma=False,
    )
```

```python
import functools

import jax
import jax.numpy as jnp
from jax import lax
from jax.experimental import pallas as pl
from jax.experimental.pallas import tpu as pltpu
from jax.sharding import PartitionSpec as P

D = 6144
HQ = 48
KVH = 8
HD = 128
FF = 8192
CTX = 384


EPSILON = 1e-05


def attend_block(queries, cache_keys, cache_values, new_keys, new_values, lengths):
    rows, kv_local = (cache_keys.shape[0], cache_keys.shape[1])
    groups = HQ // KVH
    factor = HD ** (-0.5)
    query_heads = queries.reshape(rows, kv_local, groups, HD)
    scores = (
        jnp.einsum("rkgd,rkpd->rkgp", query_heads, cache_keys, preferred_element_type=jnp.float32)
        * factor
    )
    valid = jnp.arange(CTX, dtype=jnp.int32)[None, :] < lengths[:, None]
    scores = jnp.where(valid[:, None, None, :], scores, -jnp.inf)
    key_heads = new_keys.reshape(rows, kv_local, HD)
    score_new = (
        jnp.einsum("rkgd,rkd->rkg", query_heads, key_heads, preferred_element_type=jnp.float32)
        * factor
    )
    highest = jnp.maximum(jnp.max(scores, axis=-1), score_new)
    exp_cache = jnp.exp(scores - highest[..., None])
    exp_new = jnp.exp(score_new - highest)
    totals = jnp.sum(exp_cache, axis=-1) + exp_new
    probs_cache = (exp_cache / totals[..., None]).astype(jnp.bfloat16)
    probs_new = (exp_new / totals).astype(jnp.bfloat16)
    attended = jnp.einsum(
        "rkgp,rkpd->rkgd", probs_cache, cache_values, preferred_element_type=jnp.float32
    )
    attended = attended + probs_new.astype(jnp.float32)[..., None] * new_values.reshape(
        rows, kv_local, 1, HD
    ).astype(jnp.float32)
    return attended.reshape(rows, kv_local * groups * HD).astype(jnp.bfloat16)


DEPTH = 2048
CHUNK = 512
MESH = pl.DeviceIdType.MESH


def layer_kernel(
    T,
    q_ref,
    nk_ref,
    nv_ref,
    len_ref,
    resid_ref,
    gain_ref,
    routes_ref,
    rw_ref,
    ck_hbm,
    cv_hbm,
    wo_hbm,
    wg_hbm,
    wu_hbm,
    wd_hbm,
    out_ref,
    w_buf,
    q_s,
    o_s,
    nk_s,
    nv_s,
    att_ref,
    att_all,
    full,
    hidden,
    act,
    acc,
    proj_send,
    proj_recv,
    sq_node,
    sq_all,
    sib_send,
    sib_recv,
    y_send,
    y_recv,
    z_recv,
    w_sem,
    kv_sem,
    att_s,
    att_r,
    pr_s,
    pr_r,
    sqn_s,
    sqn_r,
    sqt_s,
    sqt_r,
    ag_z_s,
    ag_y_s,
    ag_c_s,
    ag_r,
    sib_s,
    sib_r,
    y_s,
    y_r,
    z_s,
    z_r,
):
    N = 4
    R, F = resid_ref.shape
    r = lax.axis_index("rep")
    n = lax.axis_index("node")
    t = lax.axis_index("tp")
    y = n // 2
    core = n % 2
    ny = (n + 2) % N
    ns = y * 2 + (core + 1) % 2
    nd = (ns + 2) % N
    SLOTS = w_buf.shape[0]
    KB = D // DEPTH
    per_c = 2 * KB
    chunks = wg_hbm.shape[1] // CHUNK
    wo_first = SLOTS - F // CHUNK

    def tpeer(d):
        return (t + d) % T

    def npeer(d):
        return (n + d) % N

    def rows(i):
        return pl.ds(pl.multiple_of(i * R, R), R)

    def feats(i):
        return pl.ds(pl.multiple_of(i * F, F), F)

    def gu_copy(slot):
        c, k = slot // per_c, slot % per_c
        hbm = wg_hbm if k < KB else wu_hbm
        return pltpu.make_async_copy(
            hbm.at[pl.ds((k % KB) * DEPTH, DEPTH), pl.ds(c * CHUNK, CHUNK)],
            w_buf.at[slot],
            w_sem.at[slot],
        )

    def dest(q):
        return ((y + 1 - q // 2) % 2) * 2 + (core + 1 - q % 2) % 2

    def down_copy(i):
        col = dest(i // (F // CHUNK)) * F + (i % (F // CHUNK)) * CHUNK
        return pltpu.make_async_copy(
            wd_hbm.at[:, pl.ds(pl.multiple_of(col, CHUNK), CHUNK)], w_buf.at[i], w_sem.at[i]
        )

    def wo_copy(j):
        return pltpu.make_async_copy(
            wo_hbm.at[:, pl.ds(j * CHUNK, CHUNK)],
            w_buf.at[wo_first + j, pl.ds(0, F)],
            w_sem.at[wo_first + j],
        )

    def remote(src, dst, ss, rs, node, tp):
        return pltpu.make_async_remote_copy(
            src_ref=src,
            dst_ref=dst,
            send_sem=ss,
            recv_sem=rs,
            device_id=(r, node, tp),
            device_id_type=MESH,
        )

    KV = nk_ref.shape[1] // HD
    G = HQ // KVH
    PAIR = KV * CTX
    RB = DEPTH // PAIR
    LB = CHUNK // HD
    kv_slots = R // (RB * LB)
    k_first = wo_first - 2 * kv_slots
    v_first = wo_first - kv_slots

    def kv_copy(hbm, first, i):
        return pltpu.make_async_copy(
            hbm.at[pl.ds(i * RB * PAIR, RB * PAIR)],
            w_buf.at[first + i // LB, pl.ds(0, RB * PAIR), pl.ds((i % LB) * HD, HD)],
            kv_sem.at[(first - k_first) * LB + i],
        )

    for i in range(R // RB):
        kv_copy(ck_hbm, k_first, i).start()
        kv_copy(cv_hbm, v_first, i).start()
    for j in range(F // CHUNK):
        wo_copy(j).start()
    for slot in range(k_first):
        gu_copy(slot).start()

    barrier = pltpu.get_barrier_semaphore()
    for d in range(1, N):
        pl.semaphore_signal(barrier, inc=1, device_id=(r, npeer(d), t), device_id_type=MESH)
    for d in range(1, T):
        pl.semaphore_signal(barrier, inc=1, device_id=(r, n, tpeer(d)), device_id_type=MESH)
    pl.semaphore_wait(barrier, N + T - 2)

    q_s[...] = jnp.zeros_like(q_s)
    for k in range(KV):
        lanes = slice(k * HD, (k + 1) * HD)
        nk_s[:, k, :] = nk_ref[:, lanes].astype(jnp.float32)
        nv_s[:, k, :] = nv_ref[:, lanes].astype(jnp.float32)
        for g in range(G):
            h = k * G + g
            q_s[:, 8 * k + g, :] = q_ref[:, h * HD : (h + 1) * HD].astype(jnp.float32)
    positions = lax.broadcasted_iota(jnp.int32, (8 * KV, CTX), 1)
    nt = (((1,), (1,)), ((), ()))

    def per_head(ref, row):
        return jnp.concatenate(
            [jnp.broadcast_to(ref[row, k : k + 1, :], (8, HD)) for k in range(KV)], axis=0
        )

    def diagonal(parts):
        return jnp.concatenate([p[8 * k : 8 * k + 8] for k, p in enumerate(parts)], axis=0)

    def attend(s, carry):
        for b in range(LB):
            for first in (k_first, v_first):
                pltpu.make_async_copy(
                    ck_hbm.at[pl.ds(0, RB * PAIR)],
                    w_buf.at[first + s, pl.ds(0, RB * PAIR), pl.ds(b * HD, HD)],
                    kv_sem.at[(first - k_first) * LB + s * LB + b],
                ).wait()
        for b in range(LB):
            lanes = slice(b * HD, (b + 1) * HD)
            for i in range(RB):
                row = (s * LB + b) * RB + i
                q = q_s[row]
                qb = q.astype(jnp.bfloat16)
                scores = diagonal(
                    [
                        lax.dot_general(
                            qb,
                            w_buf[k_first + s, i * PAIR + k * CTX : i * PAIR + (k + 1) * CTX, lanes],
                            nt,
                            preferred_element_type=jnp.float32,
                        )
                        for k in range(KV)
                    ]
                )
                scores = scores * HD ** (-0.5)
                scores = jnp.where(positions < len_ref[row], scores, -jnp.inf)
                new = jnp.sum(q * per_head(nk_s, row), axis=1, keepdims=True) * HD ** (-0.5)
                highest = jnp.maximum(jnp.max(scores, axis=1, keepdims=True), new)
                e = jnp.exp(scores - highest)
                e_new = jnp.exp(new - highest)
                scale = 1.0 / (jnp.sum(e, axis=1, keepdims=True) + e_new)
                probs = (e * scale).astype(jnp.bfloat16)
                p_new = (e_new * scale).astype(jnp.bfloat16).astype(jnp.float32)
                o = diagonal(
                    [
                        jnp.dot(
                            probs,
                            w_buf[v_first + s, i * PAIR + k * CTX : i * PAIR + (k + 1) * CTX, lanes],
                            preferred_element_type=jnp.float32,
                        )
                        for k in range(KV)
                    ]
                )
                o_s[row] = o + p_new * per_head(nv_s, row)
        return carry

    lax.fori_loop(0, kv_slots, attend, 0)
    for k in range(KV):
        for g in range(G):
            h = k * G + g
            att_ref[:, h * HD : (h + 1) * HD] = o_s[:, 8 * k + g, :].astype(jnp.bfloat16)
    for slot in range(k_first, wo_first):
        gu_copy(slot).start()

    sends = []

    def send(*args):
        copy = remote(*args)
        copy.start()
        sends.append(copy)

    for d in (2, 1, 3):
        send(att_ref, att_all.at[rows(n)], att_s.at[d], att_r.at[n], npeer(d), t)
    att_all[rows(n), :] = att_ref[...]
    for d in range(1, N):
        p = npeer(d)
        remote(att_ref, att_all.at[rows(p)], att_s.at[d], att_r.at[p], p, t).wait_recv()

    for j in range(F // CHUNK):
        wo_copy(j).wait()
        part = jnp.dot(
            att_all[...], w_buf[wo_first + j, :F, :], preferred_element_type=jnp.float32
        )
        acc[:, j * CHUNK : (j + 1) * CHUNK] = part
        proj_send[:, j * CHUNK : (j + 1) * CHUNK] = part.astype(jnp.bfloat16)
    for d in (2, 1, 3):
        p = tpeer(d)
        send(proj_send.at[rows(p)], proj_recv.at[t], pr_s.at[d], pr_r.at[t], n, p)
    for slot in range(wo_first, SLOTS):
        gu_copy(slot).start()
    total = resid_ref[...].astype(jnp.float32) + acc[rows(t), :]
    for d in range(1, T):
        p = tpeer(d)
        remote(
            proj_send.at[rows(p)], proj_recv.at[p], pr_s.at[d], pr_r.at[p], n, p
        ).wait_recv()
        total = total + proj_recv[p].astype(jnp.float32)
    hidden[...] = total

    full[rows(t), feats(n)] = (total * gain_ref[...]).astype(jnp.bfloat16)
    sq_node[n] = jnp.broadcast_to(jnp.sum(total * total, axis=1, keepdims=True), (R, 128))
    for d in range(1, N):
        send(sq_node.at[n], sq_node.at[n], sqn_s.at[d], sqn_r.at[n], npeer(d), t)

    def block(nn, tt):
        return full.at[rows(tt), feats(nn)]

    own = block(n, t)
    send(own, own, ag_y_s.at[0], ag_r.at[n, t], ny, t)
    for d in (2, 1, 3):
        send(own, own, ag_z_s.at[d], ag_r.at[n, t], n, tpeer(d))
    send(own, own, ag_c_s.at[0, 0], ag_r.at[n, t], ns, t)

    for d in range(1, N):
        p = npeer(d)
        remote(sq_node.at[n], sq_node.at[p], sqn_s.at[d], sqn_r.at[p], p, t).wait_recv()
    sq_all[rows(t), :] = sq_node[0] + sq_node[1] + sq_node[2] + sq_node[3]
    for d in range(1, T):
        sq = sq_all.at[rows(t)]
        send(sq, sq, sqt_s.at[d], sqt_r.at[t], n, tpeer(d))

    def arrived(nn, tt):
        remote(own, block(nn, tt), ag_y_s.at[0], ag_r.at[nn, tt], ny, t).wait_recv()

    for d in (1, 3, 2):
        p = tpeer(d)
        b = block(n, p)
        arrived(n, p)
        send(b, b, ag_y_s.at[d], ag_r.at[n, p], ny, t)
        send(b, b, ag_c_s.at[0, d], ag_r.at[n, p], ns, t)
    for d in (0, 1, 3, 2):
        p = tpeer(d)
        b = block(ny, p)
        arrived(ny, p)
        send(b, b, ag_c_s.at[1, d], ag_r.at[ny, p], ns, t)
    for d in range(T):
        arrived(ns, tpeer(d))
        arrived(nd, tpeer(d))
    for d in range(1, T):
        p = tpeer(d)
        sq = sq_all.at[rows(p)]
        remote(sq, sq, sqt_s.at[d], sqt_r.at[p], n, p).wait_recv()
    inv = lax.rsqrt(sq_all[:, 0:1] / D + EPSILON)

    def slot_wait(slot):
        pltpu.make_async_copy(
            wd_hbm.at[:, pl.ds(0, CHUNK)], w_buf.at[slot], w_sem.at[slot]
        ).wait()

    downs = D // CHUNK

    def gate_up(c, carry):
        base = c * per_c
        both = []
        for m in range(2):
            s = None
            for k in range(KB):
                slot = base + m * KB + k
                slot_wait(slot)
                part = jnp.dot(
                    full[:, k * DEPTH : (k + 1) * DEPTH],
                    w_buf[slot],
                    preferred_element_type=jnp.float32,
                )
                s = part if s is None else s + part
            both.append(s * inv)
        gate, up = both
        act[:, pl.ds(pl.multiple_of(c * CHUNK, CHUNK), CHUNK)] = (
            gate / (1.0 + jnp.exp(-gate)) * up
        ).astype(jnp.bfloat16)

        @pl.when(c < downs // per_c)
        def _():
            for k in range(per_c):
                down_copy(base + k).start()

        return carry

    lax.fori_loop(0, chunks, gate_up, 0)

    expert = (n * T + t) * wg_hbm.shape[1] // FF
    weight = jnp.sum(jnp.where(routes_ref[...] == expert, rw_ref[...], 0.0), axis=1, keepdims=True)

    def down(q, store):
        def step(k, carry):
            slot = q * (F // CHUNK) + k
            slot_wait(slot)
            part = jnp.dot(act[...], w_buf[slot], preferred_element_type=jnp.float32)
            store(pl.ds(pl.multiple_of(k * CHUNK, CHUNK), CHUNK), part * weight)
            return carry

        lax.fori_loop(0, F // CHUNK, step, 0)

    def to_sibling(h):
        def store(cols, v):
            sib_send[h, :, cols] = v.astype(jnp.bfloat16)

        return store

    def to_acc(cols, v):
        acc[:, cols] = v

    def sib_wait(h):
        remote(
            sib_send.at[h], sib_recv.at[h], sib_s.at[h], sib_r.at[h], ns, t
        ).wait_recv()

    down(0, to_sibling(0))
    send(sib_send.at[0], sib_recv.at[0], sib_s.at[0], sib_r.at[0], ns, t)
    down(1, to_acc)
    sib_wait(0)
    for d in (2, 1, 3, 0):
        p = tpeer(d)
        y_send[p] = (acc[rows(p), :] + sib_recv[0, rows(p), :].astype(jnp.float32)).astype(
            jnp.bfloat16
        )
        send(y_send.at[p], y_recv.at[p], y_s.at[d], y_r.at[p], ny, t)
    down(2, to_sibling(1))
    send(sib_send.at[1], sib_recv.at[1], sib_s.at[1], sib_r.at[1], ns, t)
    down(3, to_acc)
    sib_wait(1)
    mine = None
    for d in (2, 1, 3, 0):
        p = tpeer(d)
        remote(y_send.at[p], y_recv.at[p], y_s.at[d], y_r.at[p], ny, t).wait_recv()
        s = (
            acc[rows(p), :]
            + sib_recv[1, rows(p), :].astype(jnp.float32)
            + y_recv[p].astype(jnp.float32)
        )
        if d == 0:
            mine = s + hidden[...]
        else:
            y_recv[p] = s.astype(jnp.bfloat16)
            send(y_recv.at[p], z_recv.at[t], z_s.at[d], z_r.at[t], n, p)
    for d in (1, 3, 2):
        p = tpeer(d)
        remote(y_recv.at[p], z_recv.at[p], z_s.at[d], z_r.at[p], n, p).wait_recv()
        mine = mine + z_recv[p].astype(jnp.float32)
    out_ref[...] = mine.astype(jnp.bfloat16)
    for copy in sends:
        copy.wait_send()


def fused_layer(
    queries,
    cache_keys,
    cache_values,
    new_keys,
    new_values,
    lengths,
    resid,
    wo,
    norm_gain,
    routes,
    route_weights,
    w_gate,
    w_up,
    w_down,
    tp,
):
    R, F = resid.shape
    rows = routes.shape[0]
    bf, f32 = jnp.bfloat16, jnp.float32
    vm = pl.BlockSpec(memory_space=pltpu.VMEM)
    hbm = pl.BlockSpec(memory_space=pl.ANY)
    kv = cache_keys.shape[1]
    slots = 2 * (D // DEPTH) * (w_gate.shape[1] // CHUNK)
    dma = pltpu.SemaphoreType.DMA
    return pl.pallas_call(
        functools.partial(layer_kernel, tp),
        out_shape=jax.ShapeDtypeStruct((R, F), bf),
        in_specs=[vm] * 3 + [pl.BlockSpec(memory_space=pltpu.SMEM)] + [vm] * 4 + [hbm] * 6,
        out_specs=vm,
        scratch_shapes=[
            pltpu.VMEM((slots, DEPTH, CHUNK), bf),
            pltpu.VMEM((R, 8 * kv, HD), f32),
            pltpu.VMEM((R, 8 * kv, HD), f32),
            pltpu.VMEM((R, kv, HD), f32),
            pltpu.VMEM((R, kv, HD), f32),
            pltpu.VMEM(queries.shape, bf),
            pltpu.VMEM((rows, F), bf),
            pltpu.VMEM((rows, D), bf),
            pltpu.VMEM((R, F), f32),
            pltpu.VMEM((rows, w_gate.shape[1]), bf),
            pltpu.VMEM((rows, F), f32),
            pltpu.VMEM((rows, F), bf),
            pltpu.VMEM((tp, R, F), bf),
            pltpu.VMEM((4, R, 128), f32),
            pltpu.VMEM((rows, 128), f32),
            pltpu.VMEM((2, rows, F), bf),
            pltpu.VMEM((2, rows, F), bf),
            pltpu.VMEM((tp, R, F), bf),
            pltpu.VMEM((tp, R, F), bf),
            pltpu.VMEM((tp, R, F), bf),
            dma((slots,)),
            dma((2 * (R // (DEPTH // (kv * CTX))),)),
            dma((4,)),
            dma((4,)),
            dma((tp,)),
            dma((tp,)),
            dma((4,)),
            dma((4,)),
            dma((tp,)),
            dma((tp,)),
            dma((tp,)),
            dma((tp,)),
            dma((2, tp)),
            dma((4, tp)),
            dma((2,)),
            dma((2,)),
            dma((tp,)),
            dma((tp,)),
            dma((tp,)),
            dma((tp,)),
        ],
        compiler_params=pltpu.CompilerParams(
            collective_id=0, has_side_effects=True, vmem_limit_bytes=60 * 1024 * 1024
        ),
        cost_estimate=pl.CostEstimate(
            flops=2 * rows * D * w_gate.shape[1] * 3,
            bytes_accessed=3 * D * w_gate.shape[1] * 2,
            transcendentals=rows * w_gate.shape[1],
        ),
    )(
        queries,
        new_keys,
        new_values,
        lengths,
        resid,
        norm_gain.reshape(1, F),
        routes,
        route_weights,
        cache_keys.reshape(-1, HD),
        cache_values.reshape(-1, HD),
        wo,
        w_gate,
        w_up,
        w_down,
    )


def local(
    queries,
    cache_keys,
    cache_values,
    new_keys,
    new_values,
    lengths,
    resid,
    wo,
    norm_gain,
    routes,
    route_weights,
    w_gate,
    w_up,
    w_down,
):
    if lax.axis_size("node") == 4 and lax.axis_size("tp") == 4:
        return fused_layer(
            queries,
            cache_keys,
            cache_values,
            new_keys,
            new_values,
            lengths,
            resid,
            wo,
            norm_gain,
            routes,
            route_weights,
            w_gate,
            w_up,
            w_down,
            lax.axis_size("tp"),
        )
    attended = attend_block(queries, cache_keys, cache_values, new_keys, new_values, lengths)
    gathered = lax.all_gather(attended, "node", axis=0, tiled=True)
    projected = lax.psum_scatter(
        jnp.dot(gathered, wo, preferred_element_type=jnp.float32),
        "tp",
        scatter_dimension=0,
        tiled=True,
    )
    hidden = resid.astype(jnp.float32) + projected
    squares = lax.psum(jnp.sum(hidden * hidden, axis=1), "node")
    normed = (hidden * lax.rsqrt(squares / D + EPSILON)[:, None] * norm_gain[None, :]).astype(
        jnp.bfloat16
    )
    all_rows = lax.all_gather(normed, "tp", axis=0, tiled=True)
    device = lax.axis_index("node") * lax.axis_size("tp") + lax.axis_index("tp")
    hidden_local = w_gate.shape[1]
    expert = device * hidden_local // FF
    expert_weight = jnp.sum(jnp.where(routes == expert, route_weights, 0.0), axis=1)
    full_rows = lax.all_gather(all_rows, "node", axis=1, tiled=True)
    gate = jnp.dot(full_rows, w_gate, preferred_element_type=jnp.float32)
    upward = jnp.dot(full_rows, w_up, preferred_element_type=jnp.float32)
    activ = (jax.nn.silu(gate) * upward).astype(jnp.bfloat16)
    weighted = jnp.dot(activ, w_down, preferred_element_type=jnp.float32) * expert_weight[:, None]
    slices = lax.psum_scatter(
        weighted.astype(jnp.bfloat16), "node", scatter_dimension=1, tiled=True
    ).astype(jnp.float32)
    moe_part = lax.psum_scatter(slices, "tp", scatter_dimension=0, tiled=True)
    return (hidden + moe_part).astype(jnp.bfloat16)


def solution(mesh):
    return jax.shard_map(
        local,
        mesh=mesh,
        in_specs=(
            P(("rep", "node"), "tp"),
            P(("rep", "node"), "tp", None, None),
            P(("rep", "node"), "tp", None, None),
            P(("rep", "node"), "tp"),
            P(("rep", "node"), "tp"),
            P(("rep", "node")),
            P(("rep", "tp"), "node"),
            P("tp", "node"),
            P("node"),
            P("rep", None),
            P("rep", None),
            P(None, ("node", "tp")),
            P(None, ("node", "tp")),
            P(("node", "tp"), None),
        ),
        out_specs=P(("rep", "tp"), "node"),
        check_vma=False,
    )
```

```python
import functools

import jax
import jax.numpy as jnp
from jax import lax
from jax.experimental import pallas as pl
from jax.experimental.pallas import tpu as pltpu
from jax.sharding import PartitionSpec as P

D = 6144
HQ = 48
KVH = 8
HD = 128
FF = 8192
CTX = 384


EPSILON = 1e-05


def attend_block(queries, cache_keys, cache_values, new_keys, new_values, lengths):
    rows, kv_local = (cache_keys.shape[0], cache_keys.shape[1])
    groups = HQ // KVH
    factor = HD ** (-0.5)
    query_heads = queries.reshape(rows, kv_local, groups, HD)
    scores = (
        jnp.einsum("rkgd,rkpd->rkgp", query_heads, cache_keys, preferred_element_type=jnp.float32)
        * factor
    )
    valid = jnp.arange(CTX, dtype=jnp.int32)[None, :] < lengths[:, None]
    scores = jnp.where(valid[:, None, None, :], scores, -jnp.inf)
    key_heads = new_keys.reshape(rows, kv_local, HD)
    score_new = (
        jnp.einsum("rkgd,rkd->rkg", query_heads, key_heads, preferred_element_type=jnp.float32)
        * factor
    )
    highest = jnp.maximum(jnp.max(scores, axis=-1), score_new)
    exp_cache = jnp.exp(scores - highest[..., None])
    exp_new = jnp.exp(score_new - highest)
    totals = jnp.sum(exp_cache, axis=-1) + exp_new
    probs_cache = (exp_cache / totals[..., None]).astype(jnp.bfloat16)
    probs_new = (exp_new / totals).astype(jnp.bfloat16)
    attended = jnp.einsum(
        "rkgp,rkpd->rkgd", probs_cache, cache_values, preferred_element_type=jnp.float32
    )
    attended = attended + probs_new.astype(jnp.float32)[..., None] * new_values.reshape(
        rows, kv_local, 1, HD
    ).astype(jnp.float32)
    return attended.reshape(rows, kv_local * groups * HD).astype(jnp.bfloat16)


CHUNK = 512
MESH = pl.DeviceIdType.MESH


def layer_kernel(
    T,
    att_ref,
    resid_ref,
    gain_ref,
    routes_ref,
    rw_ref,
    wo_hbm,
    wg_hbm,
    wu_hbm,
    wd_hbm,
    out_ref,
    w_buf,
    gu_acc,
    att_all,
    full,
    hidden,
    act,
    acc,
    proj_send,
    proj_recv,
    sq_node,
    sq_all,
    sib_send,
    sib_recv,
    y_send,
    y_recv,
    z_recv,
    w_sem,
    att_s,
    att_r,
    pr_s,
    pr_r,
    sqn_s,
    sqn_r,
    sqt_s,
    sqt_r,
    ag_z_s,
    ag_y_s,
    ag_c_s,
    ag_r,
    sib_s,
    sib_r,
    y_s,
    y_r,
    z_s,
    z_r,
):
    N = 4
    R, F = resid_ref.shape
    r = lax.axis_index("rep")
    n = lax.axis_index("node")
    t = lax.axis_index("tp")
    y = n // 2
    core = n % 2
    ny = (n + 2) % N
    ns = y * 2 + (core + 1) % 2
    nd = (ns + 2) % N
    SLOTS = w_buf.shape[0]
    chunks = wg_hbm.shape[1] // CHUNK
    per_k = 2 * chunks
    order = (n, ns, ny, nd)
    PARTS = F // CHUNK
    wo_first = SLOTS - F // CHUNK

    def tpeer(d):
        return (t + d) % T

    def npeer(d):
        return (n + d) % N

    def rows(i):
        return pl.ds(pl.multiple_of(i * R, R), R)

    def feats(i):
        return pl.ds(pl.multiple_of(i * F, F), F)

    def gu_copy(slot):
        c = slot % per_k // 2
        hbm = wu_hbm if slot % 2 else wg_hbm
        return pltpu.make_async_copy(
            hbm.at[feats(order[slot // per_k]), pl.ds(c * CHUNK, CHUNK)],
            w_buf.at[slot],
            w_sem.at[slot],
        )

    def dest(q):
        return ((y + 1 - q // 2) % 2) * 2 + (core + 1 - q % 2) % 2

    def down_start(slot):
        k = slot % chunks
        for j in range(PARTS):
            col = dest(slot // chunks) * F + j * CHUNK
            pltpu.make_async_copy(
                wd_hbm.at[pl.ds(k * CHUNK, CHUNK), pl.ds(pl.multiple_of(col, CHUNK), CHUNK)],
                w_buf.at[slot, pl.ds(j * CHUNK, CHUNK)],
                w_sem.at[slot],
            ).start()

    def wo_copy(j):
        return pltpu.make_async_copy(
            wo_hbm.at[:, pl.ds(j * CHUNK, CHUNK)],
            w_buf.at[wo_first + j],
            w_sem.at[wo_first + j],
        )

    def remote(src, dst, ss, rs, node, tp):
        return pltpu.make_async_remote_copy(
            src_ref=src,
            dst_ref=dst,
            send_sem=ss,
            recv_sem=rs,
            device_id=(r, node, tp),
            device_id_type=MESH,
        )

    for j in range(F // CHUNK):
        wo_copy(j).start()
    for slot in range(wo_first):
        gu_copy(slot).start()

    barrier = pltpu.get_barrier_semaphore()
    for d in range(1, N):
        pl.semaphore_signal(barrier, inc=1, device_id=(r, npeer(d), t), device_id_type=MESH)
    for d in range(1, T):
        pl.semaphore_signal(barrier, inc=1, device_id=(r, n, tpeer(d)), device_id_type=MESH)
    pl.semaphore_wait(barrier, N + T - 2)

    sends = []

    def send(*args):
        copy = remote(*args)
        copy.start()
        sends.append(copy)

    for d in (2, 1, 3):
        send(att_ref, att_all.at[rows(n)], att_s.at[d], att_r.at[n], npeer(d), t)
    att_all[rows(n), :] = att_ref[...]
    for d in range(1, N):
        p = npeer(d)
        remote(att_ref, att_all.at[rows(p)], att_s.at[d], att_r.at[p], p, t).wait_recv()

    for j in range(F // CHUNK):
        wo_copy(j).wait()
        part = jnp.dot(
            att_all[...], w_buf[wo_first + j], preferred_element_type=jnp.float32
        )
        acc[:, j * CHUNK : (j + 1) * CHUNK] = part
        proj_send[:, j * CHUNK : (j + 1) * CHUNK] = part.astype(jnp.bfloat16)
    for d in (2, 1, 3):
        p = tpeer(d)
        send(proj_send.at[rows(p)], proj_recv.at[t], pr_s.at[d], pr_r.at[t], n, p)
    for slot in range(wo_first, SLOTS):
        gu_copy(slot).start()
    total = resid_ref[...].astype(jnp.float32) + acc[rows(t), :]
    for d in range(1, T):
        p = tpeer(d)
        remote(
            proj_send.at[rows(p)], proj_recv.at[p], pr_s.at[d], pr_r.at[p], n, p
        ).wait_recv()
        total = total + proj_recv[p].astype(jnp.float32)
    hidden[...] = total

    full[rows(t), feats(n)] = (total * gain_ref[...][None, :]).astype(jnp.bfloat16)
    sq_node[n] = jnp.broadcast_to(jnp.sum(total * total, axis=1, keepdims=True), (R, 128))
    for d in range(1, N):
        send(sq_node.at[n], sq_node.at[n], sqn_s.at[d], sqn_r.at[n], npeer(d), t)

    def block(nn, tt):
        return full.at[rows(tt), feats(nn)]

    own = block(n, t)
    send(own, own, ag_y_s.at[0], ag_r.at[n, t], ny, t)
    for d in (2, 1, 3):
        send(own, own, ag_z_s.at[d], ag_r.at[n, t], n, tpeer(d))
    send(own, own, ag_c_s.at[0, 0], ag_r.at[n, t], ns, t)

    for d in range(1, N):
        p = npeer(d)
        remote(sq_node.at[n], sq_node.at[p], sqn_s.at[d], sqn_r.at[p], p, t).wait_recv()
    sq_all[rows(t), :] = sq_node[0] + sq_node[1] + sq_node[2] + sq_node[3]
    for d in range(1, T):
        sq = sq_all.at[rows(t)]
        send(sq, sq, sqt_s.at[d], sqt_r.at[t], n, tpeer(d))

    def arrived(nn, tt):
        remote(own, block(nn, tt), ag_y_s.at[0], ag_r.at[nn, tt], ny, t).wait_recv()

    for d in (1, 3, 2):
        p = tpeer(d)
        b = block(n, p)
        arrived(n, p)
        send(b, b, ag_y_s.at[d], ag_r.at[n, p], ny, t)
        send(b, b, ag_c_s.at[0, d], ag_r.at[n, p], ns, t)

    def slot_wait(slot):
        pltpu.make_async_copy(
            wo_hbm.at[:, pl.ds(0, CHUNK)], w_buf.at[slot], w_sem.at[slot]
        ).wait()

    def gate_up(k, finish=None):
        def step(c, carry):
            both = []
            for m in range(2):
                slot = k * per_k + c * 2 + m
                slot_wait(slot)
                part = jnp.dot(
                    full[:, feats(order[k])], w_buf[slot], preferred_element_type=jnp.float32
                )
                if k > 0:
                    part = gu_acc[c * 2 + m] + part
                if finish is None:
                    gu_acc[c * 2 + m] = part
                both.append(part)
            if finish is not None:
                gate, up = both[0] * finish, both[1] * finish
                act[:, pl.ds(pl.multiple_of(c * CHUNK, CHUNK), CHUNK)] = (
                    gate / (1.0 + jnp.exp(-gate)) * up
                ).astype(jnp.bfloat16)
            return carry

        lax.fori_loop(0, chunks, step, 0)
        for slot in range(k * per_k, (k + 1) * per_k):
            if slot < N * chunks:
                down_start(slot)

    gate_up(0)
    for d in (0, 1, 3, 2):
        p = tpeer(d)
        b = block(ny, p)
        arrived(ny, p)
        send(b, b, ag_c_s.at[1, d], ag_r.at[ny, p], ns, t)
    for d in range(T):
        arrived(ns, tpeer(d))
    gate_up(1)
    gate_up(2)
    for d in range(T):
        arrived(nd, tpeer(d))
    for d in range(1, T):
        p = tpeer(d)
        sq = sq_all.at[rows(p)]
        remote(sq, sq, sqt_s.at[d], sqt_r.at[p], n, p).wait_recv()
    gate_up(3, lax.rsqrt(sq_all[:, 0:1] / D + EPSILON))

    expert = (n * T + t) * wg_hbm.shape[1] // FF
    weight = jnp.sum(jnp.where(routes_ref[...] == expert, rw_ref[...], 0.0), axis=0, keepdims=True)
    square = (weight.shape[1], weight.shape[1])
    eye = lax.broadcasted_iota(jnp.int32, square, 0) == lax.broadcasted_iota(jnp.int32, square, 1)
    weight = jnp.sum(
        jnp.where(eye, jnp.broadcast_to(weight, square), 0.0), axis=1, keepdims=True
    )

    def down(q, store):
        for k in range(chunks):
            slot_wait(q * chunks + k)

        def step(j, carry):
            cols = pl.ds(pl.multiple_of(j * CHUNK, CHUNK), CHUNK)
            total = None
            for k in range(chunks):
                part = jnp.dot(
                    act[:, k * CHUNK : (k + 1) * CHUNK],
                    w_buf[q * chunks + k, cols, :],
                    preferred_element_type=jnp.float32,
                )
                total = part if total is None else total + part
            store(cols, total * weight)
            return carry

        lax.fori_loop(0, PARTS, step, 0)

    def to_sibling(h):
        def store(cols, v):
            sib_send[h, :, cols] = v.astype(jnp.bfloat16)

        return store

    def to_acc(cols, v):
        acc[:, cols] = v

    def sib_wait(h):
        remote(
            sib_send.at[h], sib_recv.at[h], sib_s.at[h], sib_r.at[h], ns, t
        ).wait_recv()

    down(0, to_sibling(0))
    send(sib_send.at[0], sib_recv.at[0], sib_s.at[0], sib_r.at[0], ns, t)
    down(1, to_acc)
    sib_wait(0)
    for d in (2, 1, 3, 0):
        p = tpeer(d)
        y_send[p] = (acc[rows(p), :] + sib_recv[0, rows(p), :].astype(jnp.float32)).astype(
            jnp.bfloat16
        )
        send(y_send.at[p], y_recv.at[p], y_s.at[d], y_r.at[p], ny, t)
    down(2, to_sibling(1))
    send(sib_send.at[1], sib_recv.at[1], sib_s.at[1], sib_r.at[1], ns, t)
    down(3, to_acc)
    sib_wait(1)
    mine = None
    for d in (2, 1, 3, 0):
        p = tpeer(d)
        remote(y_send.at[p], y_recv.at[p], y_s.at[d], y_r.at[p], ny, t).wait_recv()
        s = (
            acc[rows(p), :]
            + sib_recv[1, rows(p), :].astype(jnp.float32)
            + y_recv[p].astype(jnp.float32)
        )
        if d == 0:
            mine = s + hidden[...]
        else:
            y_recv[p] = s.astype(jnp.bfloat16)
            send(y_recv.at[p], z_recv.at[t], z_s.at[d], z_r.at[t], n, p)
    for d in (1, 3, 2):
        p = tpeer(d)
        remote(y_recv.at[p], z_recv.at[p], z_s.at[d], z_r.at[p], n, p).wait_recv()
        mine = mine + z_recv[p].astype(jnp.float32)
    out_ref[...] = mine.astype(jnp.bfloat16)
    for copy in sends:
        copy.wait_send()


def fused_layer(
    attended, resid, wo, norm_gain, routes, route_weights, w_gate, w_up, w_down, tp
):
    R, F = resid.shape
    rows = routes.shape[0]
    bf, f32 = jnp.bfloat16, jnp.float32
    vm = pl.BlockSpec(memory_space=pltpu.VMEM)
    hbm = pl.BlockSpec(memory_space=pl.ANY)
    chunks = w_gate.shape[1] // CHUNK
    slots = 2 * (D // F) * chunks
    dma = pltpu.SemaphoreType.DMA
    return pl.pallas_call(
        functools.partial(layer_kernel, tp),
        out_shape=jax.ShapeDtypeStruct((R, F), bf),
        in_specs=[vm] * 5 + [hbm] * 4,
        out_specs=vm,
        scratch_shapes=[
            pltpu.VMEM((slots, F, CHUNK), bf),
            pltpu.VMEM((2 * chunks, rows, CHUNK), f32),
            pltpu.VMEM((rows, F), bf),
            pltpu.VMEM((rows, D), bf),
            pltpu.VMEM((R, F), f32),
            pltpu.VMEM((rows, w_gate.shape[1]), bf),
            pltpu.VMEM((rows, F), f32),
            pltpu.VMEM((rows, F), bf),
            pltpu.VMEM((tp, R, F), bf),
            pltpu.VMEM((4, R, 128), f32),
            pltpu.VMEM((rows, 128), f32),
            pltpu.VMEM((2, rows, F), bf),
            pltpu.VMEM((2, rows, F), bf),
            pltpu.VMEM((tp, R, F), bf),
            pltpu.VMEM((tp, R, F), bf),
            pltpu.VMEM((tp, R, F), bf),
            dma((slots,)),
            dma((4,)),
            dma((4,)),
            dma((tp,)),
            dma((tp,)),
            dma((4,)),
            dma((4,)),
            dma((tp,)),
            dma((tp,)),
            dma((tp,)),
            dma((tp,)),
            dma((2, tp)),
            dma((4, tp)),
            dma((2,)),
            dma((2,)),
            dma((tp,)),
            dma((tp,)),
            dma((tp,)),
            dma((tp,)),
        ],
        compiler_params=pltpu.CompilerParams(
            collective_id=0, has_side_effects=True, vmem_limit_bytes=60 * 1024 * 1024
        ),
        cost_estimate=pl.CostEstimate(
            flops=2 * rows * D * w_gate.shape[1] * 3,
            bytes_accessed=3 * D * w_gate.shape[1] * 2,
            transcendentals=rows * w_gate.shape[1],
        ),
    )(
        attended,
        resid,
        norm_gain,
        routes.T,
        route_weights.T,
        wo,
        w_gate,
        w_up,
        w_down,
    )


def local(
    queries,
    cache_keys,
    cache_values,
    new_keys,
    new_values,
    lengths,
    resid,
    wo,
    norm_gain,
    routes,
    route_weights,
    w_gate,
    w_up,
    w_down,
):
    attended = attend_block(queries, cache_keys, cache_values, new_keys, new_values, lengths)
    if lax.axis_size("node") == 4 and lax.axis_size("tp") == 4:
        return fused_layer(
            attended,
            resid,
            wo,
            norm_gain,
            routes,
            route_weights,
            w_gate,
            w_up,
            w_down,
            lax.axis_size("tp"),
        )
    gathered = lax.all_gather(attended, "node", axis=0, tiled=True)
    projected = lax.psum_scatter(
        jnp.dot(gathered, wo, preferred_element_type=jnp.float32),
        "tp",
        scatter_dimension=0,
        tiled=True,
    )
    hidden = resid.astype(jnp.float32) + projected
    squares = lax.psum(jnp.sum(hidden * hidden, axis=1), "node")
    normed = (hidden * lax.rsqrt(squares / D + EPSILON)[:, None] * norm_gain[None, :]).astype(
        jnp.bfloat16
    )
    all_rows = lax.all_gather(normed, "tp", axis=0, tiled=True)
    device = lax.axis_index("node") * lax.axis_size("tp") + lax.axis_index("tp")
    hidden_local = w_gate.shape[1]
    expert = device * hidden_local // FF
    expert_weight = jnp.sum(jnp.where(routes == expert, route_weights, 0.0), axis=1)
    full_rows = lax.all_gather(all_rows, "node", axis=1, tiled=True)
    gate = jnp.dot(full_rows, w_gate, preferred_element_type=jnp.float32)
    upward = jnp.dot(full_rows, w_up, preferred_element_type=jnp.float32)
    activ = (jax.nn.silu(gate) * upward).astype(jnp.bfloat16)
    weighted = jnp.dot(activ, w_down, preferred_element_type=jnp.float32) * expert_weight[:, None]
    slices = lax.psum_scatter(
        weighted.astype(jnp.bfloat16), "node", scatter_dimension=1, tiled=True
    ).astype(jnp.float32)
    moe_part = lax.psum_scatter(slices, "tp", scatter_dimension=0, tiled=True)
    return (hidden + moe_part).astype(jnp.bfloat16)


def solution(mesh):
    return jax.shard_map(
        local,
        mesh=mesh,
        in_specs=(
            P(("rep", "node"), "tp"),
            P(("rep", "node"), "tp", None, None),
            P(("rep", "node"), "tp", None, None),
            P(("rep", "node"), "tp"),
            P(("rep", "node"), "tp"),
            P(("rep", "node")),
            P(("rep", "tp"), "node"),
            P("tp", "node"),
            P("node"),
            P("rep", None),
            P("rep", None),
            P(None, ("node", "tp")),
            P(None, ("node", "tp")),
            P(("node", "tp"), None),
        ),
        out_specs=P(("rep", "tp"), "node"),
        check_vma=False,
    )
```

```python
import functools

import jax
import jax.numpy as jnp
from jax import lax
from jax.experimental import pallas as pl
from jax.experimental.pallas import tpu as pltpu
from jax.sharding import PartitionSpec as P

D = 6144
HQ = 48
KVH = 8
HD = 128
FF = 8192
CTX = 384


EPSILON = 1e-05


def attend_block(queries, cache_keys, cache_values, new_keys, new_values, lengths):
    rows, kv_local = (cache_keys.shape[0], cache_keys.shape[1])
    groups = HQ // KVH
    factor = HD ** (-0.5)
    query_heads = queries.reshape(rows, kv_local, groups, HD)
    scores = (
        jnp.einsum("rkgd,rkpd->rkgp", query_heads, cache_keys, preferred_element_type=jnp.float32)
        * factor
    )
    valid = jnp.arange(CTX, dtype=jnp.int32)[None, :] < lengths[:, None]
    scores = jnp.where(valid[:, None, None, :], scores, -jnp.inf)
    key_heads = new_keys.reshape(rows, kv_local, HD)
    score_new = (
        jnp.einsum("rkgd,rkd->rkg", query_heads, key_heads, preferred_element_type=jnp.float32)
        * factor
    )
    highest = jnp.maximum(jnp.max(scores, axis=-1), score_new)
    exp_cache = jnp.exp(scores - highest[..., None])
    exp_new = jnp.exp(score_new - highest)
    totals = jnp.sum(exp_cache, axis=-1) + exp_new
    probs_cache = (exp_cache / totals[..., None]).astype(jnp.bfloat16)
    probs_new = (exp_new / totals).astype(jnp.bfloat16)
    attended = jnp.einsum(
        "rkgp,rkpd->rkgd", probs_cache, cache_values, preferred_element_type=jnp.float32
    )
    attended = attended + probs_new.astype(jnp.float32)[..., None] * new_values.reshape(
        rows, kv_local, 1, HD
    ).astype(jnp.float32)
    return attended.reshape(rows, kv_local * groups * HD).astype(jnp.bfloat16)


CHUNK = 512
MESH = pl.DeviceIdType.MESH


def layer_kernel(
    T,
    att_ref,
    resid_ref,
    gain_ref,
    routes_ref,
    rw_ref,
    wo_hbm,
    wg_hbm,
    wu_hbm,
    wd_hbm,
    out_ref,
    w_buf,
    gu_acc,
    att_all,
    full,
    hidden,
    act,
    acc,
    proj_send,
    proj_recv,
    sq_node,
    sq_all,
    sib_send,
    sib_recv,
    y_send,
    y_recv,
    z_recv,
    w_sem,
    att_s,
    att_r,
    pr_s,
    pr_r,
    sqn_s,
    sqn_r,
    sqt_s,
    sqt_r,
    ag_z_s,
    ag_y_s,
    ag_c_s,
    ag_r,
    sib_s,
    sib_r,
    y_s,
    y_r,
    z_s,
    z_r,
):
    N = 4
    R, F = resid_ref.shape
    r = lax.axis_index("rep")
    n = lax.axis_index("node")
    t = lax.axis_index("tp")
    y = n // 2
    core = n % 2
    ny = (n + 2) % N
    ns = y * 2 + (core + 1) % 2
    nd = (ns + 2) % N
    SLOTS = w_buf.shape[0]
    chunks = wg_hbm.shape[1] // CHUNK
    per_k = 2 * chunks
    order = (n, ns, ny, nd)
    PARTS = F // CHUNK
    wo_first = SLOTS - F // CHUNK

    def tpeer(d):
        return (t + d) % T

    def npeer(d):
        return (n + d) % N

    def rows(i):
        return pl.ds(pl.multiple_of(i * R, R), R)

    def feats(i):
        return pl.ds(pl.multiple_of(i * F, F), F)

    def gu_copy(slot):
        c = slot % per_k // 2
        hbm = wu_hbm if slot % 2 else wg_hbm
        return pltpu.make_async_copy(
            hbm.at[feats(order[slot // per_k]), pl.ds(c * CHUNK, CHUNK)],
            w_buf.at[slot],
            w_sem.at[slot],
        )

    def dest(q):
        return ((y + 1 - q // 2) % 2) * 2 + (core + 1 - q % 2) % 2

    def down_start(slot):
        k = slot % chunks
        for j in range(PARTS):
            col = dest(slot // chunks) * F + j * CHUNK
            pltpu.make_async_copy(
                wd_hbm.at[pl.ds(k * CHUNK, CHUNK), pl.ds(pl.multiple_of(col, CHUNK), CHUNK)],
                w_buf.at[slot, pl.ds(j * CHUNK, CHUNK)],
                w_sem.at[slot],
            ).start()

    def wo_copy(j):
        return pltpu.make_async_copy(
            wo_hbm.at[:, pl.ds(j * CHUNK, CHUNK)],
            w_buf.at[wo_first + j],
            w_sem.at[wo_first + j],
        )

    def remote(src, dst, ss, rs, node, tp):
        return pltpu.make_async_remote_copy(
            src_ref=src,
            dst_ref=dst,
            send_sem=ss,
            recv_sem=rs,
            device_id=(r, node, tp),
            device_id_type=MESH,
        )

    for j in range(F // CHUNK):
        wo_copy(j).start()
    for slot in range(wo_first):
        gu_copy(slot).start()

    barrier = pltpu.get_barrier_semaphore()
    for d in range(1, N):
        pl.semaphore_signal(barrier, inc=1, device_id=(r, npeer(d), t), device_id_type=MESH)
    for d in range(1, T):
        pl.semaphore_signal(barrier, inc=1, device_id=(r, n, tpeer(d)), device_id_type=MESH)
    pl.semaphore_wait(barrier, N + T - 2)

    sends = []

    def send(*args):
        copy = remote(*args)
        copy.start()
        sends.append(copy)

    for d in (2, 1, 3):
        send(att_ref, att_all.at[rows(n)], att_s.at[d], att_r.at[n], npeer(d), t)
    att_all[rows(n), :] = att_ref[...]
    for d in range(1, N):
        p = npeer(d)
        remote(att_ref, att_all.at[rows(p)], att_s.at[d], att_r.at[p], p, t).wait_recv()

    def proj_block(p, source, j):
        cols = pl.ds(j * CHUNK, CHUNK)
        return proj_send.at[rows(p), cols], proj_recv.at[source, :, cols]

    for j in range(F // CHUNK):
        wo_copy(j).wait()
        part = jnp.dot(
            att_all[...], w_buf[wo_first + j], preferred_element_type=jnp.float32
        )
        acc[:, j * CHUNK : (j + 1) * CHUNK] = part
        proj_send[:, j * CHUNK : (j + 1) * CHUNK] = part.astype(jnp.bfloat16)
        for d in (2, 1, 3):
            p = tpeer(d)
            send(*proj_block(p, t, j), pr_s.at[j, d], pr_r.at[j, t], n, p)
    for slot in range(wo_first, SLOTS):
        gu_copy(slot).start()
    total = resid_ref[...].astype(jnp.float32) + acc[rows(t), :]
    for d in range(1, T):
        p = tpeer(d)
        for j in range(PARTS):
            remote(*proj_block(p, p, j), pr_s.at[j, d], pr_r.at[j, p], n, p).wait_recv()
        total = total + proj_recv[p].astype(jnp.float32)
    hidden[...] = total

    full[rows(t), feats(n)] = (total * gain_ref[...][None, :]).astype(jnp.bfloat16)
    sq_node[n] = jnp.broadcast_to(jnp.sum(total * total, axis=1, keepdims=True), (R, 128))
    for d in range(1, N):
        send(sq_node.at[n], sq_node.at[n], sqn_s.at[d], sqn_r.at[n], npeer(d), t)

    def block(nn, tt):
        return full.at[rows(tt), feats(nn)]

    own = block(n, t)
    send(own, own, ag_y_s.at[0], ag_r.at[n, t], ny, t)
    for d in (2, 1, 3):
        send(own, own, ag_z_s.at[d], ag_r.at[n, t], n, tpeer(d))
    send(own, own, ag_c_s.at[0, 0], ag_r.at[n, t], ns, t)

    for d in range(1, N):
        p = npeer(d)
        remote(sq_node.at[n], sq_node.at[p], sqn_s.at[d], sqn_r.at[p], p, t).wait_recv()
    sq_all[rows(t), :] = sq_node[0] + sq_node[1] + sq_node[2] + sq_node[3]
    for d in range(1, T):
        sq = sq_all.at[rows(t)]
        send(sq, sq, sqt_s.at[d], sqt_r.at[t], n, tpeer(d))

    def arrived(nn, tt):
        remote(own, block(nn, tt), ag_y_s.at[0], ag_r.at[nn, tt], ny, t).wait_recv()

    for d in (1, 3, 2):
        p = tpeer(d)
        b = block(n, p)
        arrived(n, p)
        send(b, b, ag_y_s.at[d], ag_r.at[n, p], ny, t)
        send(b, b, ag_c_s.at[0, d], ag_r.at[n, p], ns, t)

    def slot_wait(slot):
        pltpu.make_async_copy(
            wo_hbm.at[:, pl.ds(0, CHUNK)], w_buf.at[slot], w_sem.at[slot]
        ).wait()

    def gate_up(k, finish=None):
        def step(c, carry):
            both = []
            for m in range(2):
                slot = k * per_k + c * 2 + m
                slot_wait(slot)
                part = jnp.dot(
                    full[:, feats(order[k])], w_buf[slot], preferred_element_type=jnp.float32
                )
                if k > 0:
                    part = gu_acc[c * 2 + m] + part
                if finish is None:
                    gu_acc[c * 2 + m] = part
                both.append(part)
            if finish is not None:
                gate, up = both[0] * finish, both[1] * finish
                act[:, pl.ds(pl.multiple_of(c * CHUNK, CHUNK), CHUNK)] = (
                    gate / (1.0 + jnp.exp(-gate)) * up
                ).astype(jnp.bfloat16)
            return carry

        lax.fori_loop(0, chunks, step, 0)
        for slot in range(k * per_k, (k + 1) * per_k):
            if slot < N * chunks:
                down_start(slot)

    gate_up(0)
    for d in (0, 1, 3, 2):
        p = tpeer(d)
        b = block(ny, p)
        arrived(ny, p)
        send(b, b, ag_c_s.at[1, d], ag_r.at[ny, p], ns, t)
    for d in range(T):
        arrived(ns, tpeer(d))
    gate_up(1)
    gate_up(2)
    for d in range(T):
        arrived(nd, tpeer(d))
    for d in range(1, T):
        p = tpeer(d)
        sq = sq_all.at[rows(p)]
        remote(sq, sq, sqt_s.at[d], sqt_r.at[p], n, p).wait_recv()
    gate_up(3, lax.rsqrt(sq_all[:, 0:1] / D + EPSILON))

    expert = (n * T + t) * wg_hbm.shape[1] // FF
    weight = jnp.sum(jnp.where(routes_ref[...] == expert, rw_ref[...], 0.0), axis=0, keepdims=True)
    square = (weight.shape[1], weight.shape[1])
    eye = lax.broadcasted_iota(jnp.int32, square, 0) == lax.broadcasted_iota(jnp.int32, square, 1)
    weight = jnp.sum(
        jnp.where(eye, jnp.broadcast_to(weight, square), 0.0), axis=1, keepdims=True
    )

    def down(q, store):
        for k in range(chunks):
            slot_wait(q * chunks + k)

        def step(j, carry):
            cols = pl.ds(pl.multiple_of(j * CHUNK, CHUNK), CHUNK)
            total = None
            for k in range(chunks):
                part = jnp.dot(
                    act[:, k * CHUNK : (k + 1) * CHUNK],
                    w_buf[q * chunks + k, cols, :],
                    preferred_element_type=jnp.float32,
                )
                total = part if total is None else total + part
            store(cols, total * weight)
            return carry

        lax.fori_loop(0, PARTS, step, 0)

    def to_sibling(h):
        def store(cols, v):
            sib_send[h, :, cols] = v.astype(jnp.bfloat16)

        return store

    def to_acc(cols, v):
        acc[:, cols] = v

    def sib_wait(h):
        remote(
            sib_send.at[h], sib_recv.at[h], sib_s.at[h], sib_r.at[h], ns, t
        ).wait_recv()

    down(0, to_sibling(0))
    send(sib_send.at[0], sib_recv.at[0], sib_s.at[0], sib_r.at[0], ns, t)
    down(1, to_acc)
    sib_wait(0)
    for d in (2, 1, 3, 0):
        p = tpeer(d)
        y_send[p] = (acc[rows(p), :] + sib_recv[0, rows(p), :].astype(jnp.float32)).astype(
            jnp.bfloat16
        )
        send(y_send.at[p], y_recv.at[p], y_s.at[d], y_r.at[p], ny, t)
    down(2, to_sibling(1))
    send(sib_send.at[1], sib_recv.at[1], sib_s.at[1], sib_r.at[1], ns, t)
    down(3, to_acc)
    sib_wait(1)
    mine = None
    for d in (2, 1, 3, 0):
        p = tpeer(d)
        remote(y_send.at[p], y_recv.at[p], y_s.at[d], y_r.at[p], ny, t).wait_recv()
        s = (
            acc[rows(p), :]
            + sib_recv[1, rows(p), :].astype(jnp.float32)
            + y_recv[p].astype(jnp.float32)
        )
        if d == 0:
            mine = s + hidden[...]
        else:
            y_recv[p] = s.astype(jnp.bfloat16)
            send(y_recv.at[p], z_recv.at[t], z_s.at[d], z_r.at[t], n, p)
    for d in (1, 3, 2):
        p = tpeer(d)
        remote(y_recv.at[p], z_recv.at[p], z_s.at[d], z_r.at[p], n, p).wait_recv()
        mine = mine + z_recv[p].astype(jnp.float32)
    out_ref[...] = mine.astype(jnp.bfloat16)
    for copy in sends:
        copy.wait_send()


def fused_layer(
    attended, resid, wo, norm_gain, routes, route_weights, w_gate, w_up, w_down, tp
):
    R, F = resid.shape
    rows = routes.shape[0]
    bf, f32 = jnp.bfloat16, jnp.float32
    vm = pl.BlockSpec(memory_space=pltpu.VMEM)
    hbm = pl.BlockSpec(memory_space=pl.ANY)
    chunks = w_gate.shape[1] // CHUNK
    slots = 2 * (D // F) * chunks
    dma = pltpu.SemaphoreType.DMA
    return pl.pallas_call(
        functools.partial(layer_kernel, tp),
        out_shape=jax.ShapeDtypeStruct((R, F), bf),
        in_specs=[vm] * 5 + [hbm] * 4,
        out_specs=vm,
        scratch_shapes=[
            pltpu.VMEM((slots, F, CHUNK), bf),
            pltpu.VMEM((2 * chunks, rows, CHUNK), f32),
            pltpu.VMEM((rows, F), bf),
            pltpu.VMEM((rows, D), bf),
            pltpu.VMEM((R, F), f32),
            pltpu.VMEM((rows, w_gate.shape[1]), bf),
            pltpu.VMEM((rows, F), f32),
            pltpu.VMEM((rows, F), bf),
            pltpu.VMEM((tp, R, F), bf),
            pltpu.VMEM((4, R, 128), f32),
            pltpu.VMEM((rows, 128), f32),
            pltpu.VMEM((2, rows, F), bf),
            pltpu.VMEM((2, rows, F), bf),
            pltpu.VMEM((tp, R, F), bf),
            pltpu.VMEM((tp, R, F), bf),
            pltpu.VMEM((tp, R, F), bf),
            dma((slots,)),
            dma((4,)),
            dma((4,)),
            dma((F // CHUNK, tp)),
            dma((F // CHUNK, tp)),
            dma((4,)),
            dma((4,)),
            dma((tp,)),
            dma((tp,)),
            dma((tp,)),
            dma((tp,)),
            dma((2, tp)),
            dma((4, tp)),
            dma((2,)),
            dma((2,)),
            dma((tp,)),
            dma((tp,)),
            dma((tp,)),
            dma((tp,)),
        ],
        compiler_params=pltpu.CompilerParams(
            collective_id=0, has_side_effects=True, vmem_limit_bytes=60 * 1024 * 1024
        ),
        cost_estimate=pl.CostEstimate(
            flops=2 * rows * D * w_gate.shape[1] * 3,
            bytes_accessed=3 * D * w_gate.shape[1] * 2,
            transcendentals=rows * w_gate.shape[1],
        ),
    )(
        attended,
        resid,
        norm_gain,
        routes.T,
        route_weights.T,
        wo,
        w_gate,
        w_up,
        w_down,
    )


def local(
    queries,
    cache_keys,
    cache_values,
    new_keys,
    new_values,
    lengths,
    resid,
    wo,
    norm_gain,
    routes,
    route_weights,
    w_gate,
    w_up,
    w_down,
):
    attended = attend_block(queries, cache_keys, cache_values, new_keys, new_values, lengths)
    if lax.axis_size("node") == 4 and lax.axis_size("tp") == 4:
        return fused_layer(
            attended,
            resid,
            wo,
            norm_gain,
            routes,
            route_weights,
            w_gate,
            w_up,
            w_down,
            lax.axis_size("tp"),
        )
    gathered = lax.all_gather(attended, "node", axis=0, tiled=True)
    projected = lax.psum_scatter(
        jnp.dot(gathered, wo, preferred_element_type=jnp.float32),
        "tp",
        scatter_dimension=0,
        tiled=True,
    )
    hidden = resid.astype(jnp.float32) + projected
    squares = lax.psum(jnp.sum(hidden * hidden, axis=1), "node")
    normed = (hidden * lax.rsqrt(squares / D + EPSILON)[:, None] * norm_gain[None, :]).astype(
        jnp.bfloat16
    )
    all_rows = lax.all_gather(normed, "tp", axis=0, tiled=True)
    device = lax.axis_index("node") * lax.axis_size("tp") + lax.axis_index("tp")
    hidden_local = w_gate.shape[1]
    expert = device * hidden_local // FF
    expert_weight = jnp.sum(jnp.where(routes == expert, route_weights, 0.0), axis=1)
    full_rows = lax.all_gather(all_rows, "node", axis=1, tiled=True)
    gate = jnp.dot(full_rows, w_gate, preferred_element_type=jnp.float32)
    upward = jnp.dot(full_rows, w_up, preferred_element_type=jnp.float32)
    activ = (jax.nn.silu(gate) * upward).astype(jnp.bfloat16)
    weighted = jnp.dot(activ, w_down, preferred_element_type=jnp.float32) * expert_weight[:, None]
    slices = lax.psum_scatter(
        weighted.astype(jnp.bfloat16), "node", scatter_dimension=1, tiled=True
    ).astype(jnp.float32)
    moe_part = lax.psum_scatter(slices, "tp", scatter_dimension=0, tiled=True)
    return (hidden + moe_part).astype(jnp.bfloat16)


def solution(mesh):
    return jax.shard_map(
        local,
        mesh=mesh,
        in_specs=(
            P(("rep", "node"), "tp"),
            P(("rep", "node"), "tp", None, None),
            P(("rep", "node"), "tp", None, None),
            P(("rep", "node"), "tp"),
            P(("rep", "node"), "tp"),
            P(("rep", "node")),
            P(("rep", "tp"), "node"),
            P("tp", "node"),
            P("node"),
            P("rep", None),
            P("rep", None),
            P(None, ("node", "tp")),
            P(None, ("node", "tp")),
            P(("node", "tp"), None),
        ),
        out_specs=P(("rep", "tp"), "node"),
        check_vma=False,
    )
```
